256 devices in a mesh: row: 8 (over x_hi, y), col: 32 (over x_lo, z, core).
Axes of the slice: x: 4 (x_hi: 2, x_lo: 2; x = x_hi * 2 + x_lo), y: 4, z: 8, core: 2. Of those that a mesh axis runs over, the one named last changes fastest.
Arguments:
- ancestor_inverse: float32 [8, 8, 2, 32, 2, 256, 256], P(None, 'row', None, 'col'), may hold values from -6 to 6
- lower_panel: float32 [2, 2, 32, 2, 256, 256], P(None, None, 'col', None, 'row'), may hold values from -0.046875 to 0.046875
- pattern: int32 [2, 64], replicated, may hold values 0 or 1
- diag_inverse: float32 [2, 2, 256, 256], P(None, None, 'col'), may hold values from -6 to 6
Outputs:
- inverse_panel: float32 [2, 256, 8, 8, 2, 256], P(None, 'col', None, 'row')
- inverse_diag: float32 [2, 2, 256, 256], P(None, None, 'col')
The draws below stay inside these ranges and needn't reach their ends.
All inputs are finite; a program needn't handle non-finite values.
Results may differ from the reference program's by a relative error of at most 0.0001.
Values sent between devices are 32-bit elements; how exact they have to be, the bound alone decides.
No kernel may reach another device: no remote copies, remote signals or barrier semaphores. Data moves between devices by JAX's collectives and lax.ppermute only.
A program may use at most 128 MiB of HBM per device.

```python
import jax
import jax.numpy as jnp
from jax import lax

W = 256
NB = 64
N_ROW = 8
N_COL = 32


def set_ends(values, stream_key, smallest, high):
    extent = values.shape
    spot = [jax.random.randint(jax.random.fold_in(stream_key, axis), (), 0, extent[axis]) for axis in range(len(extent))]
    values = values.at[tuple(spot)].set(smallest)
    longest = extent.index(max(extent))
    spot[longest] = (spot[longest] + 1) % extent[longest]
    return values.at[tuple(spot)].set(high)


def level_of(stream_key, dims, cuts, least, high):
    gain = 1.0
    for axis_at, shards_of in cuts:
        steps = jax.random.uniform(jax.random.fold_in(jax.random.fold_in(stream_key, 6), axis_at), (shards_of,), jnp.float32, least / len(cuts), high / len(cuts))
        gain = gain * jnp.repeat(jnp.exp(steps), dims[axis_at] // shards_of).reshape((-1,) + (1,) * (len(dims) - 1 - axis_at))
    return gain


def gaussian(rng, shape, width, most, cuts=(), dtype=jnp.bfloat16):
    values = jax.random.normal(rng, shape, jnp.float32) * width
    if len(cuts) > 0:
        values = level_of(rng, shape, cuts, -0.22, 0.18) * values
    return jnp.clip(values, min=-most, max=most).astype(dtype)


def setup_inputs(seed: int = 0) -> dict:
    arg_keys = jax.random.split(jax.random.key(seed), 5)
    return {
        "ancestor_inverse": gaussian(arg_keys[0], (NB // N_ROW, N_ROW, NB // N_COL, N_COL, 2, W, W), 1.0, 6.0, ((1, 8), (3, 32)), jnp.float32),
        "lower_panel": gaussian(arg_keys[1], (2, NB // N_COL, N_COL, 2, W, W), (NB * W) ** -0.5, 0.046875, ((2, 32), (4, 8)), jnp.float32),
        "pattern": set_ends((jax.random.randint(arg_keys[2], (2, NB), 0, 2) < 1).astype(jnp.int32), jax.random.fold_in(arg_keys[2], 1), 0, 1),
        "diag_inverse": gaussian(arg_keys[3], (2, 2, W, W), 1.0, 6.0, ((2, 32),), jnp.float32),
    }


PRECISE = lax.Precision.HIGHEST


def matmul(left, right):
    return jnp.dot(left, right, precision=PRECISE, preferred_element_type=jnp.float32)


def reference(ancestor_inverse, lower_panel, pattern, diag_inverse):
    blocks = ancestor_inverse.reshape(NB, NB, 2, W, W)
    factor = lower_panel.reshape(2, NB, 2, W, W)
    struct_mask = pattern.astype(jnp.float32)
    panels = []
    diags = []
    for which in range(2):
        masked = factor[which] * struct_mask[which][:, None, None, None]
        flat_real = masked[:, 0].reshape(NB * W, W)
        flat_imag = masked[:, 1].reshape(NB * W, W)

        def block_row(row_blocks):
            row_real = jnp.transpose(row_blocks[:, 0], (1, 0, 2)).reshape(W, NB * W)
            row_imag = jnp.transpose(row_blocks[:, 1], (1, 0, 2)).reshape(W, NB * W)
            real_part = matmul(row_imag, flat_imag) - matmul(row_real, flat_real)
            imag_part = -(matmul(row_real, flat_imag) + matmul(row_imag, flat_real))
            return jnp.stack((real_part, imag_part))

        result = lax.map(block_row, blocks)
        result = result * struct_mask[which][:, None, None, None]
        result_real = result[:, 0].reshape(NB * W, W)
        result_imag = result[:, 1].reshape(NB * W, W)
        diag_real = diag_inverse[which, 0] - (matmul(flat_real.T, result_real) - matmul(flat_imag.T, result_imag))
        diag_imag = diag_inverse[which, 1] - (matmul(flat_real.T, result_imag) + matmul(flat_imag.T, result_real))
        diags.append(jnp.stack((diag_real, diag_imag)))
        panels.append(jnp.transpose(result.reshape(NB // N_ROW, N_ROW, 2, W, W), (3, 0, 1, 2, 4)))
    return jnp.stack(panels), jnp.stack(diags)
```

```python
import functools

import jax
import jax.numpy as jnp
from jax import lax
from jax.experimental import pallas as pl
from jax.experimental.pallas import tpu as pltpu
from jax.sharding import Mesh, PartitionSpec as P

W = 256
F32 = jnp.float32
BF16 = jnp.bfloat16
SWAP = [(0, 1), (1, 0)]
ROW = ("xh", "y")
COL = ("xl", "zh", "zl", "co")
Z = ("zh", "zl")
EVERY = ROW + COL


def split(values):
    high = values.astype(BF16)
    low = (values - high.astype(F32)).astype(BF16)
    return high, low


def product_kernel(slot_ref, keep_ref, *refs):
    pieces = refs[:8]
    own_ref, other_ref, out_ref, right_hi, right_lo, left_hi, left_lo = refs[8:]

    @pl.when(pl.program_id(0) == 0)
    def _():
        for s in range(8):
            first = pl.multiple_of(slot_ref[s] * 32, 32)
            for block in range(4):
                real = split(pieces[s][block, 0])
                imag = split(pieces[s][block, 1])
                top = pl.ds(block * 512 + first, 32)
                bottom = pl.ds(block * 512 + 256 + first, 32)
                for part, target in ((0, right_hi), (1, right_lo)):
                    target[top, 0:256] = -real[part]
                    target[top, 256:512] = -imag[part]
                    target[bottom, 0:256] = imag[part]
                    target[bottom, 256:512] = -real[part]

    for at, source in ((0, own_ref), (1, other_ref)):
        for b in range(2):
            for t in range(2):
                high, low = split(source[0, b, t])
                cols = pl.ds(((at * 2 + b) * 2 + t) * 256, 256)
                left_hi[:, cols] = high
                left_lo[:, cols] = low
    dot = functools.partial(jnp.dot, preferred_element_type=F32)
    total = dot(left_hi[...], right_hi[...])
    total += dot(left_hi[...], right_lo[...])
    total += dot(left_lo[...], right_hi[...])
    total = total * keep_ref[pl.program_id(0)]
    for z in range(8):
        for x in range(2):
            rows = (x * 8 + z) * 16
            for t in range(2):
                out_ref[z, 0, t, x] = total[rows:rows + 16, t * 256:(t + 1) * 256]


def products(slots, keep, pieces, own, other):
    whole = pl.BlockSpec((4, 2, 32, W), lambda i: (0, 0, 0, 0))
    block = pl.BlockSpec((1, 2, 2, W, W), lambda i: (i, 0, 0, 0, 0))
    smem = pl.BlockSpec(memory_space=pltpu.SMEM)
    return pl.pallas_call(
        product_kernel,
        grid=(8,),
        in_specs=[smem, smem] + [whole] * 8 + [block, block],
        out_specs=pl.BlockSpec((8, 1, 2, 2, 16, W), lambda i: (0, i, 0, 0, 0, 0)),
        out_shape=jax.ShapeDtypeStruct((8, 8, 2, 2, 16, W), F32),
        scratch_shapes=[
            pltpu.VMEM((2048, 512), BF16),
            pltpu.VMEM((2048, 512), BF16),
            pltpu.VMEM((W, 2048), BF16),
            pltpu.VMEM((W, 2048), BF16),
        ],
        compiler_params=pltpu.CompilerParams(vmem_limit_bytes=40 * 1024 * 1024),
        cost_estimate=pl.CostEstimate(
            flops=3 * 2 * 8 * 256 * 2048 * 512, bytes_accessed=24 << 20, transcendentals=0
        ),
    )(slots, keep, *pieces, own, other)


def diag_kernel(factor_ref, panel_ref, out_ref, fr, fi, xr, xi):
    for a in range(8):
        for x in range(2):
            rows = pl.ds((a * 2 + x) * 16, 16)
            fr[rows] = factor_ref[x * 4 + a % 4, a // 4, 0]
            fi[rows] = factor_ref[x * 4 + a % 4, a // 4, 1]
            xr[rows] = panel_ref[a, 0, x]
            xi[rows] = panel_ref[a, 1, x]
    fr2, fi2 = split(fr[...]), split(fi[...])
    xr2, xi2 = split(xr[...]), split(xi[...])

    def mul(left, right):
        def dot(p, q):
            return lax.dot_general(
                p, q, (((0,), (0,)), ((), ())), preferred_element_type=F32
            )

        return dot(left[0], right[0]) + dot(left[0], right[1]) + dot(left[1], right[0])

    real = mul(fr2, xr2) - mul(fi2, xi2)
    imag = mul(fr2, xi2) + mul(fi2, xr2)
    for d in range(16):
        out_ref[d, 0] = real[d * 16:(d + 1) * 16]
        out_ref[d, 1] = imag[d * 16:(d + 1) * 16]


def diag_terms(factor, panel):
    vmem = pl.BlockSpec(memory_space=pltpu.VMEM)
    return pl.pallas_call(
        diag_kernel,
        in_specs=[vmem, vmem],
        out_specs=vmem,
        out_shape=jax.ShapeDtypeStruct((16, 2, 16, W), F32),
        scratch_shapes=[pltpu.VMEM((W, W), F32)] * 4,
        compiler_params=pltpu.CompilerParams(vmem_limit_bytes=40 * 1024 * 1024),
        cost_estimate=pl.CostEstimate(
            flops=3 * 8 * 256**3, bytes_accessed=3 << 19, transcendentals=0
        ),
    )(factor, panel)


def relocation():
    pairs = []
    for r in range(8):
        for c in range(32):
            xh, y = divmod(r, 4)
            xs, zs, cs = c // 16, c // 2 % 8, c % 2
            row = zs % 4 * 2 + cs
            col = xh * 16 + (y * 2 + xs) * 2 + zs // 4
            pairs.append((r * 32 + c, row * 32 + col))
    return pairs


def on_device(ancestor_inverse, lower_panel, pattern, diag_inverse):
    mask = pattern.astype(F32)
    core = lax.axis_index("co")
    row = lax.axis_index(ROW)
    col = lax.axis_index(COL)
    owned = ancestor_inverse.reshape(8, 2, 2, W, W)
    lower = lower_panel.reshape(2, 2, 2, 32, W)
    mask_cols = lax.dynamic_index_in_dim(mask.reshape(2, 2, 32), col, 2, keepdims=False)
    masked = lower * mask_cols[:, :, None, None, None]
    mine = lax.dynamic_index_in_dim(masked, core, 0, keepdims=False)
    theirs = lax.dynamic_index_in_dim(masked, 1 - core, 0, keepdims=False)
    received = lax.ppermute(theirs, "co", SWAP)
    shard = jnp.concatenate((mine, received))
    pieces = [shard]
    for s in range(1, 8):
        pieces.append(lax.ppermute(shard, ROW, [(i, i ^ s) for i in range(8)]))
    slots = jnp.bitwise_xor(row, jnp.arange(8, dtype=jnp.int32))
    sibling = lax.ppermute(owned, "co", SWAP)
    keep = lax.dynamic_index_in_dim(mask, core, 0, keepdims=False).reshape(8, 8)
    keep = lax.dynamic_index_in_dim(keep, row, 1, keepdims=False)
    partial = products(slots, keep, pieces, owned, sibling)

    masked, partial = lax.optimization_barrier((masked, partial))
    panel = lax.psum_scatter(
        partial.reshape(8, 512, W), Z, scatter_dimension=0, tiled=True
    ).reshape(8, 2, 2, 16, W)

    moved = lax.ppermute(masked, EVERY, relocation())
    moved = moved.reshape(2, 2, 2, 2, 16, W).transpose(3, 0, 1, 2, 4, 5)
    moved = jnp.broadcast_to(moved, (2,) + moved.shape).reshape(8, 2, 2, 16, W)
    factor = lax.all_to_all(moved, ("xl", "zl", "co"), 0, 0, tiled=True)

    terms = diag_terms(factor, panel)
    terms = lax.all_to_all(terms, ("xl",) + Z, 0, 0, tiled=True).sum(0)
    terms = terms.reshape(2, 2, 8, W).transpose(1, 0, 2, 3)
    terms = jnp.broadcast_to(terms, (8,) + terms.shape).reshape(16, 2, 8, W)
    terms = lax.all_to_all(terms, ROW + ("co",), 0, 0, tiled=True)
    inverse_diag = diag_inverse - terms.reshape(8, 2, 2, 8, W).sum(0)

    here = lax.axis_index("xl")
    keep_half = lax.dynamic_index_in_dim(panel, here, 2, keepdims=False)
    send_half = lax.dynamic_index_in_dim(panel, 1 - here, 2, keepdims=False)
    half = keep_half + lax.ppermute(send_half, "xl", SWAP)
    half = half.reshape(8, 2, 2, 8, W)
    keep_rows = lax.dynamic_index_in_dim(half, core, 2, keepdims=False)
    send_rows = lax.dynamic_index_in_dim(half, 1 - core, 2, keepdims=False)
    other_rows = lax.ppermute(send_rows, "co", SWAP)
    first = jnp.where(core == 0, keep_rows, other_rows)
    second = jnp.where(core == 0, other_rows, keep_rows)
    inverse_panel = jnp.stack((first, second)).transpose(0, 3, 1, 2, 4)[:, :, :, None]
    return (inverse_panel, inverse_diag)


def solution(mesh):
    fine = Mesh(
        mesh.devices.reshape(2, 4, 2, 4, 2, 2), EVERY
    )
    in_specs = (
        P(None, ROW, None, COL, None, None, None),
        P(None, None, COL, None, ROW, None),
        P(),
        P(None, None, COL, None),
    )
    out_specs = (P(None, COL, None, ROW, None, None), P(None, None, COL, None))
    return jax.shard_map(
        on_device, mesh=fine, in_specs=in_specs, out_specs=out_specs, check_vma=False
    )
```

```python
import functools

import jax
import jax.numpy as jnp
from jax import lax
from jax.experimental import pallas as pl
from jax.experimental.pallas import tpu as pltpu
from jax.sharding import Mesh, PartitionSpec as P

W = 256
CHAINS = 4
F32 = jnp.float32
BF16 = jnp.bfloat16
SWAP = [(0, 1), (1, 0)]
ROW = ("xh", "y")
COL = ("xl", "zh", "zl", "co")
EVERY = ROW + COL
VMEM_LIMIT = 28 * 1024 * 1024


def split(values):
    high = values.astype(BF16)
    low = (values - high.astype(F32)).astype(BF16)
    return high, low


def split_kernel(block_ref, high_ref, low_ref):
    for b in range(2):
        real = block_ref[0, b, 0]
        imag = block_ref[0, b, 1]
        cols = pl.ds(b * W, W)
        for m, part in enumerate((real, imag, real + imag)):
            high_ref[0, m, :, cols], low_ref[0, m, :, cols] = split(part)


def split_blocks(owned):
    out = pl.BlockSpec((1, 3, W, 2 * W), lambda i: (i, 0, 0, 0))
    shape = jax.ShapeDtypeStruct((8, 3, W, 2 * W), BF16)
    return pl.pallas_call(
        split_kernel,
        grid=(8,),
        in_specs=[pl.BlockSpec((1, 2, 2, W, W), lambda i: (i, 0, 0, 0, 0))],
        out_specs=[out, out],
        out_shape=[shape, shape],
        compiler_params=pltpu.CompilerParams(vmem_limit_bytes=VMEM_LIMIT),
        cost_estimate=pl.CostEstimate(flops=1 << 22, bytes_accessed=20 << 20, transcendentals=0),
    )(owned)


def prepare_kernel(slot_ref, *refs):
    pieces = refs[:8]
    high_ref, low_ref = refs[8:]
    for s in range(8):
        for b in range(2):
            rows = pl.ds(pl.multiple_of(slot_ref[s] * 32 + b * W, 32), 32)
            for k in range(2):
                real = pieces[s][k, b, 0]
                imag = pieces[s][k, b, 1]
                cols = pl.ds(k * W, W)
                for m, part in enumerate((real, imag, real + imag)):
                    high_ref[m, rows, cols], low_ref[m, rows, cols] = split(part)


def prepare(slots, pieces):
    vmem = pl.BlockSpec(memory_space=pltpu.VMEM)
    smem = pl.BlockSpec(memory_space=pltpu.SMEM)
    shape = jax.ShapeDtypeStruct((3, 2 * W, 2 * W), BF16)
    return pl.pallas_call(
        prepare_kernel,
        in_specs=[smem] + [vmem] * 8,
        out_specs=[vmem, vmem],
        out_shape=[shape, shape],
        compiler_params=pltpu.CompilerParams(vmem_limit_bytes=VMEM_LIMIT),
        cost_estimate=pl.CostEstimate(flops=1 << 20, bytes_accessed=6 << 20, transcendentals=0),
    )(slots, *pieces)


def product_kernel(core_ref, place_ref, keep_ref, *refs):
    left_hi, left_lo, right_hi, right_lo, theirs_ref, mine_ref = refs
    dot = functools.partial(jnp.dot, preferred_element_type=F32)
    core = core_ref[0]

    def store(out_ref, which, i, real, imag):
        for z in range(8):
            at = place_ref[which, z]
            for x in range(2):
                rows = (x * 8 + z) * 16
                out_ref[at, i, 0, x] = real[rows:rows + 16]
                out_ref[at, i, 1, x] = imag[rows:rows + 16]

    def multiply(i, cols):
        def product(m):
            total = dot(left_hi[i, m], right_hi[m, :, cols])
            total += dot(left_hi[i, m], right_lo[m, :, cols])
            return total + dot(left_lo[i, m], right_hi[m, :, cols])

        rr, ii, ss = product(0), product(1), product(2)
        return ii - rr, rr + ii - ss

    for i in range(2):
        first, second = keep_ref[0, i] != 0, keep_ref[1, i] != 0

        @pl.when(first & second)
        def _():
            real, imag = multiply(i, pl.ds(0, 2 * W))
            for k in range(2):
                cols = slice(k * W, (k + 1) * W)

                @pl.when(core == k)
                def _():
                    store(mine_ref, 0, i, real[:, cols], imag[:, cols])

                @pl.when(core != k)
                def _():
                    store(theirs_ref, 1, i, real[:, cols], imag[:, cols])

        @pl.when(first != second)
        def _():
            k = jnp.where(first, 0, 1)
            real, imag = multiply(i, pl.ds(pl.multiple_of(k * W, W), W))

            @pl.when(core == k)
            def _():
                store(mine_ref, 0, i, real, imag)

            @pl.when(core != k)
            def _():
                store(theirs_ref, 1, i, real, imag)

        for which, out_ref in ((0, mine_ref), (1, theirs_ref)):

            @pl.when(keep_ref[core ^ which, i] == 0)
            def _():
                out_ref[:, i] = jnp.zeros((8, 2, 2, 16, W), F32)


def products(chain, core, place, keep, left, right):
    smem = pl.BlockSpec(memory_space=pltpu.SMEM)
    block = pl.BlockSpec((2, 3, W, 2 * W), lambda c: (chain, 0, 0, 0))
    whole = pl.BlockSpec((3, 2 * W, 2 * W), lambda c: (0, 0, 0))
    out = pl.BlockSpec((8, 2, 2, 2, 16, W), lambda c: (0, 0, 0, 0, 0, 0))
    shape = jax.ShapeDtypeStruct((8, 2, 2, 2, 16, W), F32)
    return pl.pallas_call(
        product_kernel,
        grid=(1,),
        in_specs=[smem, smem, smem, block, block, whole, whole],
        out_specs=[out, out],
        out_shape=[shape, shape],
        compiler_params=pltpu.CompilerParams(vmem_limit_bytes=VMEM_LIMIT),
        cost_estimate=pl.CostEstimate(
            flops=9 * 2 * 512**3, bytes_accessed=8 << 20, transcendentals=0
        ),
    )(core, place, keep, *left, *right)


def diag_kernel(bits_ref, *refs):
    factors = refs[:2]
    panels = refs[2:2 + CHAINS]
    out_ref, fr, fi, xr, xi = refs[2 + CHAINS:]
    for number in range(8):
        i, j = number // 2 % 2, number % 2
        x = (number // 4) ^ bits_ref[0]
        m = (j ^ bits_ref[2]) * 2 + (i ^ bits_ref[1])
        for b in range(2):
            rows = pl.ds(pl.multiple_of(((b * 4 + m) * 2 + x) * 16, 16), 16)
            fr[rows] = factors[number // 4][i, j, b, 0]
            fi[rows] = factors[number // 4][i, j, b, 1]
    for a in range(8):
        for x in range(2):
            rows = pl.ds((a * 2 + x) * 16, 16)
            xr[rows] = panels[a // 2][a % 2, 0, x]
            xi[rows] = panels[a // 2][a % 2, 1, x]
    fr2, fi2 = split(fr[...]), split(fi[...])
    xr2, xi2 = split(xr[...]), split(xi[...])

    def mul(left, right):
        def dot(p, q):
            return lax.dot_general(
                p, q, (((0,), (0,)), ((), ())), preferred_element_type=F32
            )

        return dot(left[0], right[0]) + dot(left[0], right[1]) + dot(left[1], right[0])

    real = mul(fr2, xr2) - mul(fi2, xi2)
    imag = mul(fr2, xi2) + mul(fi2, xr2)
    for d in range(16):
        out_ref[d, 0] = real[d * 16:(d + 1) * 16]
        out_ref[d, 1] = imag[d * 16:(d + 1) * 16]


def diag_terms(bits, factors, panels):
    vmem = pl.BlockSpec(memory_space=pltpu.VMEM)
    return pl.pallas_call(
        diag_kernel,
        in_specs=[pl.BlockSpec(memory_space=pltpu.SMEM)] + [vmem] * (2 + CHAINS),
        out_specs=vmem,
        out_shape=jax.ShapeDtypeStruct((16, 2, 16, W), F32),
        scratch_shapes=[pltpu.VMEM((W, W), F32)] * 4,
        compiler_params=pltpu.CompilerParams(vmem_limit_bytes=VMEM_LIMIT),
        cost_estimate=pl.CostEstimate(
            flops=3 * 8 * 256**3, bytes_accessed=3 << 19, transcendentals=0
        ),
    )(bits, *factors, *panels)


def relocation():
    pairs = []
    for r in range(8):
        for c in range(32):
            xh, y = divmod(r, 4)
            xs, zs, cs = c // 16, c // 2 % 8, c % 2
            row = zs % 4 * 2 + cs
            col = xh * 16 + (y * 2 + zs // 4) * 2 + xs
            pairs.append((r * 32 + c, row * 32 + col))
    return pairs


def ring():
    pairs = []
    for z in range(8):
        for core in range(2):
            pairs.append((z * 2 + core, (z + 1 - 2 * core) % 8 * 2 + core))
    return pairs


def pick(values, index, axis=0):
    return lax.dynamic_index_in_dim(values, index, axis, keepdims=False)


def matching_factor(moved, core, z_low):
    given = lax.ppermute(pick(moved, 1 - core), "co", SWAP)
    held = jnp.stack((pick(moved, core), given)).reshape(2, 2, 2, 2, 16, W)
    given = lax.ppermute(pick(held, 1 - z_low, 3), "zl", SWAP)
    held = jnp.stack((pick(held, z_low, 3), given))
    return held, lax.ppermute(held, "xl", SWAP)


def on_device(ancestor_inverse, lower_panel, pattern, diag_inverse):
    mask = pattern.astype(F32)
    core = lax.axis_index("co")
    x_low = lax.axis_index("xl")
    z_low = lax.axis_index("zl")
    z = lax.axis_index(("zh", "zl"))
    y = lax.axis_index("y")
    x_high = lax.axis_index("xh")
    row = lax.axis_index(ROW)
    col = lax.axis_index(COL)
    owned = ancestor_inverse.reshape(8, 2, 2, W, W)
    lower = lower_panel.reshape(2, 2, 2, 32, W)
    mask_cols = pick(mask.reshape(2, 2, 32), col, 2)
    masked = lower * mask_cols[:, :, None, None, None]

    across = lax.ppermute(masked, "xh", SWAP)

    def around(block):
        turns = [[(i, (i + s) % 4) for i in range(4)] for s in (1, 3, 2)]
        return [block] + [lax.ppermute(block, "y", turn) for turn in turns]

    pieces = around(masked) + around(across)
    turned = (y - jnp.array([0, 1, 3, 2], jnp.int32)) % 4
    slots = jnp.concatenate((turned + 4 * x_high, turned + 4 * (1 - x_high)))
    left = split_blocks(lax.optimization_barrier((owned, across))[0])
    right = prepare(slots, pieces)
    moved = lax.ppermute(masked, EVERY, relocation())
    right, moved = lax.optimization_barrier((right, moved))
    factors = matching_factor(moved, core, z_low)

    away = z - jnp.arange(8, dtype=jnp.int32)
    sign = 1 - 2 * core
    place = jnp.stack(((sign * away - 1) % 8, (-sign * away - 1) % 8))
    keep = pick(pattern.reshape(2, 8, 8), row, 2)
    panels = []
    for chain in range(CHAINS):
        theirs, mine = products(
            chain, core.reshape(1), place, keep[:, 2 * chain:2 * chain + 2], left, right
        )
        given = lax.ppermute(theirs, "co", SWAP)
        panel = mine[0] + given[0]
        for step in range(1, 8):
            panel = lax.ppermute(panel, ("zh", "zl", "co"), ring()) + (mine[step] + given[step])
        panels.append(panel)

    bits = jnp.stack((x_low, z_low, core)).astype(jnp.int32)
    terms = diag_terms(bits, factors, panels)
    terms = lax.all_to_all(terms, ("xl", "zh", "zl"), 0, 0, tiled=True).sum(0)
    terms, *panels = lax.optimization_barrier((terms, *panels))
    terms = terms.reshape(2, 2, 8, W).transpose(1, 0, 2, 3)
    terms = jnp.broadcast_to(terms, (8,) + terms.shape).reshape(16, 2, 8, W)
    terms = lax.all_to_all(terms, ROW + ("co",), 0, 0, tiled=True)
    inverse_diag = diag_inverse - terms.reshape(8, 2, 2, 8, W).sum(0)

    panel = jnp.concatenate(panels)
    joined = pick(panel, x_low, 2) + lax.ppermute(pick(panel, 1 - x_low, 2), "xl", SWAP)
    joined = joined.reshape(8, 2, 2, 8, W)
    mine = pick(joined, core, 2)
    given = lax.ppermute(pick(joined, 1 - core, 2), "co", SWAP)
    both = jnp.stack((jnp.where(core == 0, mine, given), jnp.where(core == 0, given, mine)))
    inverse_panel = both.transpose(0, 3, 1, 2, 4)[:, :, :, None]
    return (inverse_panel, inverse_diag)


def solution(mesh):
    fine = Mesh(mesh.devices.reshape(2, 4, 2, 4, 2, 2), EVERY)
    in_specs = (
        P(None, ROW, None, COL, None, None, None),
        P(None, None, COL, None, ROW, None),
        P(),
        P(None, None, COL, None),
    )
    out_specs = (P(None, COL, None, ROW, None, None), P(None, None, COL, None))
    return jax.shard_map(
        on_device, mesh=fine, in_specs=in_specs, out_specs=out_specs, check_vma=False
    )
```

```python
import functools

import jax
import jax.numpy as jnp
from jax import lax
from jax.experimental import pallas as pl
from jax.experimental.pallas import tpu as pltpu
from jax.sharding import Mesh, PartitionSpec as P

W = 256
CHAINS = 4
F32 = jnp.float32
BF16 = jnp.bfloat16
SWAP = [(0, 1), (1, 0)]
ROW = ("xh", "y")
COL = ("xl", "zh", "zl", "co")
EVERY = ROW + COL
VMEM_LIMIT = 28 * 1024 * 1024


def split(values):
    high = values.astype(BF16)
    low = (values - high.astype(F32)).astype(BF16)
    return high, low


def split_kernel(block_ref, high_ref, low_ref):
    for b in range(2):
        real = block_ref[0, b, 0]
        imag = block_ref[0, b, 1]
        cols = pl.ds(b * W, W)
        for m, part in enumerate((real, imag, real + imag)):
            high_ref[0, m, :, cols], low_ref[0, m, :, cols] = split(part)


def split_blocks(owned):
    out = pl.BlockSpec((1, 3, W, 2 * W), lambda i: (i, 0, 0, 0))
    shape = jax.ShapeDtypeStruct((8, 3, W, 2 * W), BF16)
    return pl.pallas_call(
        split_kernel,
        grid=(8,),
        in_specs=[pl.BlockSpec((1, 2, 2, W, W), lambda i: (i, 0, 0, 0, 0))],
        out_specs=[out, out],
        out_shape=[shape, shape],
        compiler_params=pltpu.CompilerParams(vmem_limit_bytes=VMEM_LIMIT),
        cost_estimate=pl.CostEstimate(flops=1 << 22, bytes_accessed=20 << 20, transcendentals=0),
    )(owned)


def prepare_kernel(slot_ref, mask_ref, *refs):
    pieces = refs[:8]
    high_ref, low_ref = refs[8:]
    for s in range(8):
        for b in range(2):
            rows = pl.ds(pl.multiple_of(slot_ref[s] * 32 + b * W, 32), 32)
            for k in range(2):
                real = pieces[s][k, b, 0] * mask_ref[k, b]
                imag = pieces[s][k, b, 1] * mask_ref[k, b]
                cols = pl.ds(k * W, W)
                for m, part in enumerate((real, imag, real + imag)):
                    high_ref[m, rows, cols], low_ref[m, rows, cols] = split(part)


def prepare(slots, mask, pieces):
    vmem = pl.BlockSpec(memory_space=pltpu.VMEM)
    smem = pl.BlockSpec(memory_space=pltpu.SMEM)
    shape = jax.ShapeDtypeStruct((3, 2 * W, 2 * W), BF16)
    return pl.pallas_call(
        prepare_kernel,
        in_specs=[smem, smem] + [vmem] * 8,
        out_specs=[vmem, vmem],
        out_shape=[shape, shape],
        compiler_params=pltpu.CompilerParams(vmem_limit_bytes=VMEM_LIMIT),
        cost_estimate=pl.CostEstimate(flops=1 << 20, bytes_accessed=6 << 20, transcendentals=0),
    )(slots, mask, *pieces)


def product_kernel(core_ref, place_ref, keep_ref, *refs):
    left_hi, left_lo, right_hi, right_lo, theirs_ref, mine_ref = refs
    dot = functools.partial(jnp.dot, preferred_element_type=F32)
    core = core_ref[0]

    def store(out_ref, which, real, imag):
        for z in range(8):
            at = place_ref[which, z]
            for x in range(2):
                rows = (x * 8 + z) * 16
                out_ref[at, 0, 0, x] = real[rows:rows + 16]
                out_ref[at, 0, 1, x] = imag[rows:rows + 16]

    def multiply(cols):
        def product(m):
            total = dot(left_hi[0, m], right_hi[m, :, cols])
            total += dot(left_hi[0, m], right_lo[m, :, cols])
            return total + dot(left_lo[0, m], right_hi[m, :, cols])

        rr, ii, ss = product(0), product(1), product(2)
        return ii - rr, rr + ii - ss

    i = pl.program_id(0)
    first, second = keep_ref[0, i] != 0, keep_ref[1, i] != 0

    @pl.when(first & second)
    def _():
        real, imag = multiply(pl.ds(0, 2 * W))
        for k in range(2):
            cols = slice(k * W, (k + 1) * W)

            @pl.when(core == k)
            def _():
                store(mine_ref, 0, real[:, cols], imag[:, cols])

            @pl.when(core != k)
            def _():
                store(theirs_ref, 1, real[:, cols], imag[:, cols])

    @pl.when(first != second)
    def _():
        k = jnp.where(first, 0, 1)
        real, imag = multiply(pl.ds(pl.multiple_of(k * W, W), W))

        @pl.when(core == k)
        def _():
            store(mine_ref, 0, real, imag)

        @pl.when(core != k)
        def _():
            store(theirs_ref, 1, real, imag)

    for which, out_ref in ((0, mine_ref), (1, theirs_ref)):

        @pl.when(keep_ref[core ^ which, i] == 0)
        def _():
            out_ref[...] = jnp.zeros((8, 1, 2, 2, 16, W), F32)


def products(chain, core, place, keep, left, right):
    smem = pl.BlockSpec(memory_space=pltpu.SMEM)
    block = pl.BlockSpec((1, 3, W, 2 * W), lambda i: (2 * chain + i, 0, 0, 0))
    whole = pl.BlockSpec((3, 2 * W, 2 * W), lambda i: (0, 0, 0))
    out = pl.BlockSpec((8, 1, 2, 2, 16, W), lambda i: (0, i, 0, 0, 0, 0))
    shape = jax.ShapeDtypeStruct((8, 2, 2, 2, 16, W), F32)
    return pl.pallas_call(
        product_kernel,
        grid=(2,),
        in_specs=[smem, smem, smem, block, block, whole, whole],
        out_specs=[out, out],
        out_shape=[shape, shape],
        compiler_params=pltpu.CompilerParams(vmem_limit_bytes=VMEM_LIMIT),
        cost_estimate=pl.CostEstimate(
            flops=9 * 2 * 512**3, bytes_accessed=8 << 20, transcendentals=0
        ),
    )(core, place, keep, *left, *right)


def diag_kernel(bits_ref, *refs):
    factors = refs[:2]
    panels = refs[2:2 + CHAINS]
    out_ref, fr, fi, xr, xi = refs[2 + CHAINS:]
    for number in range(8):
        i, j = number // 2 % 2, number % 2
        x = j ^ bits_ref[2]
        m = ((number // 4) ^ bits_ref[0]) * 2 + (i ^ bits_ref[1])
        for b in range(2):
            rows = pl.ds(pl.multiple_of(((b * 4 + m) * 2 + x) * 16, 16), 16)
            fr[rows] = factors[number // 4][i, j, b, 0]
            fi[rows] = factors[number // 4][i, j, b, 1]
    for a in range(8):
        for x in range(2):
            rows = pl.ds((a * 2 + x) * 16, 16)
            xr[rows] = panels[a // 2][a % 2, 0, x]
            xi[rows] = panels[a // 2][a % 2, 1, x]
    fr2, fi2 = split(fr[...]), split(fi[...])
    xr2, xi2 = split(xr[...]), split(xi[...])

    def mul(left, right):
        def dot(p, q):
            return lax.dot_general(
                p, q, (((0,), (0,)), ((), ())), preferred_element_type=F32
            )

        return dot(left[0], right[0]) + dot(left[0], right[1]) + dot(left[1], right[0])

    real = mul(fr2, xr2) - mul(fi2, xi2)
    imag = mul(fr2, xi2) + mul(fi2, xr2)
    for d in range(16):
        out_ref[d, 0] = real[d * 16:(d + 1) * 16]
        out_ref[d, 1] = imag[d * 16:(d + 1) * 16]


def diag_terms(bits, factors, panels):
    vmem = pl.BlockSpec(memory_space=pltpu.VMEM)
    return pl.pallas_call(
        diag_kernel,
        in_specs=[pl.BlockSpec(memory_space=pltpu.SMEM)] + [vmem] * (2 + CHAINS),
        out_specs=vmem,
        out_shape=jax.ShapeDtypeStruct((16, 2, 16, W), F32),
        scratch_shapes=[pltpu.VMEM((W, W), F32)] * 4,
        compiler_params=pltpu.CompilerParams(vmem_limit_bytes=VMEM_LIMIT),
        cost_estimate=pl.CostEstimate(
            flops=3 * 8 * 256**3, bytes_accessed=3 << 19, transcendentals=0
        ),
    )(bits, *factors, *panels)


def relocation():
    pairs = []
    for r in range(8):
        for c in range(32):
            xh, y = divmod(r, 4)
            xs, zs, cs = c // 16, c // 2 % 8, c % 2
            row = zs % 4 * 2 + cs
            col = xs * 16 + ((y + zs % 4) % 4 * 2 + zs // 4) * 2 + xh
            pairs.append((r * 32 + c, row * 32 + col))
    return pairs


def unturn():
    pairs = []
    for r in range(8):
        for z in range(4):
            pairs.append((r * 4 + z, r * 4 + (z - r // 2) % 4))
    return pairs


def ring():
    pairs = []
    for z in range(8):
        for core in range(2):
            pairs.append((z * 2 + core, (z + 1 - 2 * core) % 8 * 2 + core))
    return pairs


def pick(values, index, axis=0):
    return lax.dynamic_index_in_dim(values, index, axis, keepdims=False)


def on_device(ancestor_inverse, lower_panel, pattern, diag_inverse):
    mask = pattern.astype(F32)
    core = lax.axis_index("co")
    x_low = lax.axis_index("xl")
    z_low = lax.axis_index("zl")
    z = lax.axis_index(("zh", "zl"))
    y = lax.axis_index("y")
    x_high = lax.axis_index("xh")
    row = lax.axis_index(ROW)
    col = lax.axis_index(COL)
    owned = ancestor_inverse.reshape(8, 2, 2, W, W)
    lower = lower_panel.reshape(2, 2, 2, 32, W)
    mask_cols = pick(mask.reshape(2, 2, 32), col, 2)

    across = lax.ppermute(lower, "xh", SWAP)

    def turn(block, steps):
        return lax.ppermute(block, "y", [(i, (i + steps) % 4) for i in range(4)])

    pieces = [lower, turn(lower, 1), turn(lower, 3), turn(lower, 2)]
    pieces += [across, turn(across, 1), turn(across, 3)]
    pieces += [lax.ppermute(pieces[3], "xh", SWAP)]
    turned = (y - jnp.array([0, 1, 3, 2], jnp.int32)) % 4
    slots = jnp.concatenate((turned + 4 * x_high, turned + 4 * (1 - x_high)))
    left = split_blocks(lax.optimization_barrier((owned, across))[0])
    right = prepare(slots, mask_cols, pieces)
    moved = lax.ppermute(lower, EVERY, relocation())
    moved = lax.ppermute(moved, ROW + ("zh",), unturn())
    right, moved = lax.optimization_barrier((right, moved))
    given = lax.ppermute(pick(moved, 1 - core), "co", SWAP)
    held = jnp.stack((pick(moved, core), given)).reshape(2, 2, 2, 2, 16, W)
    held, away_held = pick(held, z_low, 3), pick(held, 1 - z_low, 3)

    away = z - jnp.arange(8, dtype=jnp.int32)
    sign = 1 - 2 * core
    place = jnp.stack(((sign * away - 1) % 8, (-sign * away - 1) % 8))
    keep = pick(pattern.reshape(2, 8, 8), row, 2)
    panels = []
    for chain in range(CHAINS):
        if chain == 1:
            right, away_held = lax.optimization_barrier((right, away_held))
            held = jnp.stack((held, lax.ppermute(away_held, "zl", SWAP)))
        if chain == 3:
            right, held = lax.optimization_barrier((right, held))
            factors = held, lax.ppermute(held, "xl", SWAP)
        theirs, mine = products(
            chain, core.reshape(1), place, keep[:, 2 * chain:2 * chain + 2], left, right
        )
        given = lax.ppermute(theirs, "co", SWAP)
        panel = mine[0] + given[0]
        for step in range(1, 8):
            panel = lax.ppermute(panel, ("zh", "zl", "co"), ring()) + (mine[step] + given[step])
        panels.append(panel)

    bits = jnp.stack((x_low, z_low, core)).astype(jnp.int32)
    terms = diag_terms(bits, factors, panels)
    terms = lax.all_to_all(terms, ("xl", "zh", "zl"), 0, 0, tiled=True).sum(0)
    terms, *panels = lax.optimization_barrier((terms, *panels))
    terms = terms.reshape(2, 2, 8, W).transpose(1, 0, 2, 3)
    terms = jnp.broadcast_to(terms, (8,) + terms.shape).reshape(16, 2, 8, W)
    terms = lax.all_to_all(terms, ROW + ("co",), 0, 0, tiled=True)
    inverse_diag = diag_inverse - terms.reshape(8, 2, 2, 8, W).sum(0)

    panel = jnp.concatenate(panels)
    joined = pick(panel, x_low, 2) + lax.ppermute(pick(panel, 1 - x_low, 2), "xl", SWAP)
    joined = joined.reshape(8, 2, 2, 8, W)
    mine = pick(joined, core, 2)
    given = lax.ppermute(pick(joined, 1 - core, 2), "co", SWAP)
    both = jnp.stack((jnp.where(core == 0, mine, given), jnp.where(core == 0, given, mine)))
    inverse_panel = both.transpose(0, 3, 1, 2, 4)[:, :, :, None]
    return (inverse_panel, inverse_diag)


def solution(mesh):
    fine = Mesh(mesh.devices.reshape(2, 4, 2, 4, 2, 2), EVERY)
    in_specs = (
        P(None, ROW, None, COL, None, None, None),
        P(None, None, COL, None, ROW, None),
        P(),
        P(None, None, COL, None),
    )
    out_specs = (P(None, COL, None, ROW, None, None), P(None, None, COL, None))
    return jax.shard_map(
        on_device, mesh=fine, in_specs=in_specs, out_specs=out_specs, check_vma=False
    )
```

```python
import functools

import jax
import jax.numpy as jnp
from jax import lax
from jax.experimental import pallas as pl
from jax.experimental.pallas import tpu as pltpu
from jax.sharding import Mesh, PartitionSpec as P

W = 256
CHAINS = 4
F32 = jnp.float32
BF16 = jnp.bfloat16
SWAP = [(0, 1), (1, 0)]
ROW = ("xh", "y")
COL = ("xl", "zh", "zl", "co")
EVERY = ROW + COL
VMEM_LIMIT = 28 * 1024 * 1024


def split(values):
    high = values.astype(BF16)
    low = (values - high.astype(F32)).astype(BF16)
    return high, low


def split_kernel(block_ref, high_ref, low_ref):
    for b in range(2):
        real = block_ref[0, b, 0]
        imag = block_ref[0, b, 1]
        cols = pl.ds(b * W, W)
        for m, part in enumerate((real, imag, real + imag)):
            high_ref[0, m, :, cols], low_ref[0, m, :, cols] = split(part)


def split_blocks(owned):
    out = pl.BlockSpec((1, 3, W, 2 * W), lambda i: (i, 0, 0, 0))
    shape = jax.ShapeDtypeStruct((8, 3, W, 2 * W), BF16)
    return pl.pallas_call(
        split_kernel,
        grid=(8,),
        in_specs=[pl.BlockSpec((1, 2, 2, W, W), lambda i: (i, 0, 0, 0, 0))],
        out_specs=[out, out],
        out_shape=[shape, shape],
        compiler_params=pltpu.CompilerParams(vmem_limit_bytes=VMEM_LIMIT),
        cost_estimate=pl.CostEstimate(flops=1 << 22, bytes_accessed=20 << 20, transcendentals=0),
    )(owned)


def prepare_kernel(slot_ref, mask_ref, *refs):
    pieces = refs[:8]
    high_ref, low_ref = refs[8:]
    for s in range(8):
        for b in range(2):
            rows = pl.ds(pl.multiple_of(slot_ref[s] * 32 + b * W, 32), 32)
            for k in range(2):
                real = pieces[s][k, b, 0] * mask_ref[k, b]
                imag = pieces[s][k, b, 1] * mask_ref[k, b]
                cols = pl.ds(k * W, W)
                for m, part in enumerate((real, imag, real + imag)):
                    high_ref[m, rows, cols], low_ref[m, rows, cols] = split(part)


def prepare(slots, mask, pieces):
    vmem = pl.BlockSpec(memory_space=pltpu.VMEM)
    smem = pl.BlockSpec(memory_space=pltpu.SMEM)
    shape = jax.ShapeDtypeStruct((3, 2 * W, 2 * W), BF16)
    return pl.pallas_call(
        prepare_kernel,
        in_specs=[smem, smem] + [vmem] * 8,
        out_specs=[vmem, vmem],
        out_shape=[shape, shape],
        compiler_params=pltpu.CompilerParams(vmem_limit_bytes=VMEM_LIMIT),
        cost_estimate=pl.CostEstimate(flops=1 << 20, bytes_accessed=6 << 20, transcendentals=0),
    )(slots, mask, *pieces)


def product_kernel(core_ref, place_ref, keep_ref, *refs):
    left_hi, left_lo, right_hi, right_lo, theirs_ref, mine_ref = refs
    dot = functools.partial(jnp.dot, preferred_element_type=F32)
    core = core_ref[0]

    i = pl.program_id(0)

    def store(out_ref, which, real, imag):
        for z in range(4):
            at = place_ref[which, 2 * z + i]
            for x in range(2):
                rows = x * 128 + z * 32
                out_ref[at, 0, x] = real[rows:rows + 32]
                out_ref[at, 1, x] = imag[rows:rows + 32]

    def multiply(cols):
        def product(m):
            total = dot(left_hi[0, m], right_hi[m, :, cols])
            total += dot(left_hi[0, m], right_lo[m, :, cols])
            return total + dot(left_lo[0, m], right_hi[m, :, cols])

        rr, ii, ss = product(0), product(1), product(2)
        return ii - rr, rr + ii - ss

    first, second = keep_ref[0, i] != 0, keep_ref[1, i] != 0

    @pl.when(first & second)
    def _():
        real, imag = multiply(pl.ds(0, 2 * W))
        for k in range(2):
            cols = slice(k * W, (k + 1) * W)

            @pl.when(core == k)
            def _():
                store(mine_ref, 0, real[:, cols], imag[:, cols])

            @pl.when(core != k)
            def _():
                store(theirs_ref, 1, real[:, cols], imag[:, cols])

    @pl.when(first != second)
    def _():
        k = jnp.where(first, 0, 1)
        real, imag = multiply(pl.ds(pl.multiple_of(k * W, W), W))

        @pl.when(core == k)
        def _():
            store(mine_ref, 0, real, imag)

        @pl.when(core != k)
        def _():
            store(theirs_ref, 1, real, imag)

    for which, out_ref in ((0, mine_ref), (1, theirs_ref)):

        @pl.when(keep_ref[core ^ which, i] == 0)
        def _():
            for z in range(4):
                out_ref[place_ref[which, 2 * z + i]] = jnp.zeros((2, 2, 32, W), F32)


def products(chain, core, place, keep, left, right):
    smem = pl.BlockSpec(memory_space=pltpu.SMEM)
    block = pl.BlockSpec((1, 3, W, 2 * W), lambda i: (2 * chain + i, 0, 0, 0))
    whole = pl.BlockSpec((3, 2 * W, 2 * W), lambda i: (0, 0, 0))
    out = pl.BlockSpec((8, 2, 2, 32, W), lambda i: (0, 0, 0, 0, 0))
    shape = jax.ShapeDtypeStruct((8, 2, 2, 32, W), F32)
    return pl.pallas_call(
        product_kernel,
        grid=(2,),
        in_specs=[smem, smem, smem, block, block, whole, whole],
        out_specs=[out, out],
        out_shape=[shape, shape],
        compiler_params=pltpu.CompilerParams(vmem_limit_bytes=VMEM_LIMIT),
        cost_estimate=pl.CostEstimate(
            flops=9 * 2 * 512**3, bytes_accessed=8 << 20, transcendentals=0
        ),
    )(core, place, keep, *left, *right)


def diag_kernel(bits_ref, *refs):
    factors = refs[:2]
    panels = refs[2:2 + CHAINS]
    out_ref, fr, fi, xr, xi = refs[2 + CHAINS:]
    for number in range(8):
        i, j, b = number // 4, number // 2 % 2, number % 2
        chain = b * 2 + (i ^ bits_ref[0])
        rows = pl.ds(pl.multiple_of((chain * 2 + (j ^ bits_ref[1])) * 32, 32), 32)
        fr[rows] = factors[i][j, b, 0]
        fi[rows] = factors[i][j, b, 1]
    for chain in range(CHAINS):
        for x in range(2):
            rows = pl.ds((chain * 2 + x) * 32, 32)
            xr[rows] = panels[chain][0, x]
            xi[rows] = panels[chain][1, x]
    fr2, fi2 = split(fr[...]), split(fi[...])
    xr2, xi2 = split(xr[...]), split(xi[...])

    def mul(left, right):
        def dot(p, q):
            return lax.dot_general(
                p, q, (((0,), (0,)), ((), ())), preferred_element_type=F32
            )

        return dot(left[0], right[0]) + dot(left[0], right[1]) + dot(left[1], right[0])

    real = mul(fr2, xr2) - mul(fi2, xi2)
    imag = mul(fr2, xi2) + mul(fi2, xr2)
    for d in range(16):
        out_ref[d, 0] = real[d * 16:(d + 1) * 16]
        out_ref[d, 1] = imag[d * 16:(d + 1) * 16]


def diag_terms(bits, factors, panels):
    vmem = pl.BlockSpec(memory_space=pltpu.VMEM)
    return pl.pallas_call(
        diag_kernel,
        in_specs=[pl.BlockSpec(memory_space=pltpu.SMEM)] + [vmem] * (2 + CHAINS),
        out_specs=vmem,
        out_shape=jax.ShapeDtypeStruct((16, 2, 16, W), F32),
        scratch_shapes=[pltpu.VMEM((W, W), F32)] * 4,
        compiler_params=pltpu.CompilerParams(vmem_limit_bytes=VMEM_LIMIT),
        cost_estimate=pl.CostEstimate(
            flops=3 * 8 * 256**3, bytes_accessed=3 << 19, transcendentals=0
        ),
    )(bits, *factors, *panels)


def relocation():
    pairs = []
    for r in range(8):
        for c in range(32):
            xh, y = divmod(r, 4)
            xs, zs, cs = c // 16, c // 2 % 8, c % 2
            row = zs % 4 * 2 + cs
            col = xs * 16 + ((y + zs % 4) % 4 * 2 + zs // 4) * 2 + xh
            pairs.append((r * 32 + c, row * 32 + col))
    return pairs


def unturn():
    pairs = []
    for r in range(8):
        for z in range(4):
            pairs.append((r * 4 + z, r * 4 + (z - r // 2) % 4))
    return pairs


def ring():
    pairs = []
    for z in range(8):
        for core in range(2):
            pairs.append((z * 2 + core, (z + 1 - 2 * core) % 8 * 2 + core))
    return pairs


def pick(values, index, axis=0):
    return lax.dynamic_index_in_dim(values, index, axis, keepdims=False)


def on_device(ancestor_inverse, lower_panel, pattern, diag_inverse):
    mask = pattern.astype(F32)
    core = lax.axis_index("co")
    x_low = lax.axis_index("xl")
    z_low = lax.axis_index("zl")
    z = lax.axis_index(("zh", "zl"))
    y = lax.axis_index("y")
    x_high = lax.axis_index("xh")
    row = lax.axis_index(ROW)
    col = lax.axis_index(COL)
    owned = ancestor_inverse.reshape(8, 2, 2, W, W)
    lower = lower_panel.reshape(2, 2, 2, 32, W)
    mask_cols = pick(mask.reshape(2, 2, 32), col, 2)

    across = lax.ppermute(lower, "xh", SWAP)

    def turn(block, steps):
        return lax.ppermute(block, "y", [(i, (i + steps) % 4) for i in range(4)])

    pieces = [lower, turn(lower, 1), turn(lower, 3), turn(lower, 2)]
    pieces += [across, turn(across, 1), turn(across, 3)]
    pieces += [lax.ppermute(pieces[3], "xh", SWAP)]
    turned = (y - jnp.array([0, 1, 3, 2], jnp.int32)) % 4
    slots = jnp.concatenate((turned + 4 * x_high, turned + 4 * (1 - x_high)))
    left = split_blocks(lax.optimization_barrier((owned, across))[0])
    right = prepare(slots, mask_cols, pieces)
    moved = lax.ppermute(lower, EVERY, relocation())
    moved = lax.ppermute(moved, ROW + ("zh",), unturn())
    right, moved = lax.optimization_barrier((right, moved))
    given = lax.ppermute(pick(moved, 1 - core), "co", SWAP)
    held = jnp.stack((pick(moved, core), given))
    away = z - jnp.arange(8, dtype=jnp.int32)
    sign = 1 - 2 * core
    place = jnp.stack(((sign * away - 1) % 8, (-sign * away - 1) % 8))
    keep = pick(pattern.reshape(2, 8, 8), row, 2)
    panels = []
    for chain in range(CHAINS):
        if chain == 1:
            right, held = lax.optimization_barrier((right, held))
            factors = held, lax.ppermute(held, "xl", SWAP)
        theirs, mine = products(
            chain, core.reshape(1), place, keep[:, 2 * chain:2 * chain + 2], left, right
        )
        given = lax.ppermute(theirs, "co", SWAP)
        panel = mine[0] + given[0]
        for step in range(1, 8):
            panel = lax.ppermute(panel, ("zh", "zl", "co"), ring()) + (mine[step] + given[step])
        panels.append(panel)

    bits = jnp.stack((x_low, core)).astype(jnp.int32)
    terms = diag_terms(bits, factors, panels)
    terms = lax.all_to_all(terms, ("xl", "zh", "zl"), 0, 0, tiled=True).sum(0)
    panel = jnp.stack(panels)
    joined = pick(panel, x_low, 2) + lax.ppermute(pick(panel, 1 - x_low, 2), "xl", SWAP)
    terms, joined = lax.optimization_barrier((terms, joined))
    terms = terms.reshape(2, 2, 8, W).transpose(1, 0, 2, 3)
    terms = jnp.broadcast_to(terms, (8,) + terms.shape).reshape(16, 2, 8, W)
    terms = lax.all_to_all(terms, ROW + ("co",), 0, 0, tiled=True)
    inverse_diag = diag_inverse - terms.reshape(8, 2, 2, 8, W).sum(0)

    joined = joined.reshape(CHAINS, 2, 2, 16, W)
    mine = pick(joined, z_low, 2)
    given = lax.ppermute(pick(joined, 1 - z_low, 2), "zl", SWAP)
    joined = jnp.stack(
        (jnp.where(z_low == 0, mine, given), jnp.where(z_low == 0, given, mine)), axis=1
    )
    joined = joined.reshape(8, 2, 2, 8, W)
    mine = pick(joined, core, 2)
    given = lax.ppermute(pick(joined, 1 - core, 2), "co", SWAP)
    both = jnp.stack((jnp.where(core == 0, mine, given), jnp.where(core == 0, given, mine)))
    inverse_panel = both.transpose(0, 3, 1, 2, 4)[:, :, :, None]
    return (inverse_panel, inverse_diag)


def solution(mesh):
    fine = Mesh(mesh.devices.reshape(2, 4, 2, 4, 2, 2), EVERY)
    in_specs = (
        P(None, ROW, None, COL, None, None, None),
        P(None, None, COL, None, ROW, None),
        P(),
        P(None, None, COL, None),
    )
    out_specs = (P(None, COL, None, ROW, None, None), P(None, None, COL, None))
    return jax.shard_map(
        on_device, mesh=fine, in_specs=in_specs, out_specs=out_specs, check_vma=False
    )
```
